32 devices in a mesh: dp: 4 (over z), mp: 8 (over y, x, core).
Axes of the slice: x: 2, y: 2, z: 4, core: 2. Of those that a mesh axis runs over, the one named last changes fastest.
Arguments:
- guess_vectors: bfloat16 [128, 16, 4096], P(('dp', 'mp')), may hold values from -6 to 6
- preceding_symbol_vector: bfloat16 [128, 4096], P(('dp', 'mp')), may hold values from -6 to 6
- earlier_memory_matrix: float32 [128, 64, 64, 64], P('dp', 'mp'), may hold values from -4 to 4
- lag_blend_factor: float32 [4096], replicated, may hold values from 0 to 1
- constant_lag_blends: float32 [5, 4096], replicated, may hold values from 0 to 1
- blending_lower_matrix: bfloat16 [4096, 160], replicated, may hold values from -0.09375 to 0.09375
- blending_raise_matrix: bfloat16 [5, 32, 4096], replicated, may hold values from -1 to 1
- constant_fading: float32 [4096], P('mp'), may hold values from -6 to -1
- fading_lower_matrix: bfloat16 [4096, 64], replicated, may hold values from -0.09375 to 0.09375
- fading_raise_matrix: bfloat16 [64, 4096], P(None, 'mp'), may hold values from -1 to 1
- diagonal_boost: float32 [64, 64], P('mp'), may hold values from -3 to 3
- acceptor_matrix: bfloat16 [4096, 4096], P('dp', 'mp'), may hold values from -0.09375 to 0.09375
- lookup_matrix: bfloat16 [4096, 4096], P('dp', 'mp'), may hold values from -0.09375 to 0.09375
- payload_matrix: bfloat16 [4096, 4096], P('dp', 'mp'), may hold values from -0.09375 to 0.09375
- gating_matrix: bfloat16 [4096, 4096], P('dp', 'mp'), may hold values from -0.09375 to 0.09375
- emission_matrix: bfloat16 [4096, 4096], P('mp', 'dp'), may hold values from -0.09375 to 0.09375
- groupwise_scaling_factor: float32 [4096], P('mp'), may hold values from 0.1 to 1.9
- groupwise_scaling_offset: float32 [4096], P('mp'), may hold values from -3 to 3
- usable_guess_amount: int32 [128], replicated, may hold values from 1 to 16, as said below
- approved_guesses: int32 [128], replicated, may hold values from 0 to 16, as said below
- destination_slot: int32 [128], replicated, may hold values from 0 to 127, as said below
Outputs:
- layer_out: bfloat16 [128, 16, 4096], P(('dp', 'mp'))
- next_state: float32 [128, 64, 64, 64], P('dp', 'mp')
- next_edge: bfloat16 [128, 4096], P('dp', 'mp')
The draws below stay inside these ranges and needn't reach their ends.
Inputs may be any that keep to these rules, and one draw needn't show every extreme that they name: `usable_guess_amount`: some request has all 16 draft tokens valid. approved_guesses[b] <= usable_guess_amount[b]; some request accepts all 16. destination_slot is a permutation of the requests. Of the 32 requests of one aligned block, at most 16 have owner slots in one aligned block of 32 slots, and some pair of blocks reaches 16.
All inputs are finite; a program needn't handle non-finite values.
Results may differ from the reference program's by a relative error of at most 0.007.
Values may be sent and summed in bfloat16 or wider, within the bound.
A program may use at most 256 MiB of HBM per device.

```python
import jax
import jax.numpy as jnp
from jax import lax

MODEL_WIDTH = 4096
ATTENTION_GROUPS = 64
GROUP_DIMENSION = 64
MIXING_INNER = 32
DECAY_INNER = 64
DRAFT = 16
REQ = 128
REQ_ROW = 32
N_MP = 8


def length_pair(key):
    first_key, second_key, forced_key, accept_key = jax.random.split(jax.random.fold_in(key, 7), 4)
    first_draw = jax.random.randint(first_key, (REQ,), 1, DRAFT + 1)
    second_draw = jax.random.randint(second_key, (REQ,), 1, DRAFT + 1)
    lengths = jnp.maximum(1, first_draw * second_draw // DRAFT)
    forced = jax.random.randint(forced_key, (), 0, REQ)
    positions = jnp.arange(REQ)
    lengths = jnp.where(positions == forced, DRAFT, lengths)
    accepted_now = jax.random.randint(accept_key, (REQ,), 0, lengths + 1)
    accepted_now = jnp.where(positions == forced, DRAFT, accepted_now)
    return (lengths.astype(jnp.int32), accepted_now.astype(jnp.int32))


def draw_usable_guess_amount(key, part):
    return length_pair(key)[0]


def draw_approved_guesses(key, part):
    return length_pair(key)[1]


def draw_destination_slot(key, part):
    groups = REQ // REQ_ROW
    mean_count = REQ_ROW // groups
    order_key, spare_key, place_key, slot_key = jax.random.split(jax.random.fold_in(key, 11), 4)
    order = jax.random.permutation(order_key, groups)
    spare = jax.random.randint(spare_key, (), 0, mean_count + 1)
    by_rank = jnp.full((groups,), mean_count, jnp.int32)
    by_rank = by_rank.at[0].set(2 * mean_count).at[1].set(spare).at[2].set(mean_count - spare)
    weights = jnp.zeros((groups,), jnp.int32).at[order].set(by_rank)
    bounds = jnp.cumsum(weights)
    placed = jax.vmap(lambda single: jax.random.permutation(single, REQ_ROW))(jax.random.split(place_key, groups))
    shift_of = jnp.sum((placed[:, :, None] >= bounds[None, None, :]).astype(jnp.int32), axis=-1)
    source = jnp.arange(groups)[:, None]
    target = (source + shift_of) % groups
    slot_perm = jax.vmap(lambda single: jax.random.permutation(single, REQ_ROW))(jax.random.split(slot_key, groups))
    slots = target * REQ_ROW + slot_perm[target, placed]
    return slots.reshape(REQ).astype(jnp.int32)


def block_scale(stream_key, extent, cuts, least, largest):
    def one(dim, shards_of):
        draws = jax.random.uniform(jax.random.fold_in(jax.random.fold_in(stream_key, 6), dim), (shards_of,), jnp.float32, least / len(cuts), largest / len(cuts))
        return jnp.repeat(jnp.exp(draws), extent[dim] // shards_of).reshape((-1,) + (1,) * (len(extent) - dim - 1))

    level = one(*cuts[0])
    for cut in cuts[1:]:
        level = level * one(*cut)
    return level


def scatter_about(stream_key, shape, deviation, limit, cuts=(), kind=jnp.bfloat16):
    array = deviation * jax.random.normal(stream_key, shape, jnp.float32)
    if cuts:
        array = array * block_scale(stream_key, shape, cuts, -0.22, 0.18)
    return jnp.clip(array, -limit, limit).astype(kind)


def setup_inputs(seed: int = 0) -> dict:
    splits = jax.random.split(jax.random.key(seed), 22)
    return {
        "guess_vectors": scatter_about(splits[0], (REQ, DRAFT, MODEL_WIDTH), 1.0, 6.0, ((0, 32),)),
        "preceding_symbol_vector": scatter_about(splits[1], (REQ, MODEL_WIDTH), 1.0, 6.0, ((0, 32),)),
        "earlier_memory_matrix": scatter_about(splits[2], (REQ, ATTENTION_GROUPS, GROUP_DIMENSION, GROUP_DIMENSION), 0.5, 4.0, ((0, 4), (1, 8)), jnp.float32),
        "lag_blend_factor": jnp.clip(jax.random.uniform(splits[3], (MODEL_WIDTH,), jnp.float32, 0.0, 1.0), 0.0, 1.0),
        "constant_lag_blends": jnp.clip(jax.random.uniform(splits[4], (5, MODEL_WIDTH), jnp.float32, 0.0, 1.0), 0.0, 1.0),
        "blending_lower_matrix": scatter_about(splits[5], (MODEL_WIDTH, 5 * MIXING_INNER), MODEL_WIDTH ** -0.5, 0.09375),
        "blending_raise_matrix": scatter_about(splits[6], (5, MIXING_INNER, MODEL_WIDTH), 0.15, 1.0),
        "constant_fading": jnp.clip(-6.0 + 5.0 * jax.random.uniform(splits[7], (MODEL_WIDTH,), jnp.float32) ** block_scale(splits[7], (MODEL_WIDTH,), ((0, 8),), -0.2, 0.2), -6.0, -1.0),
        "fading_lower_matrix": scatter_about(splits[8], (MODEL_WIDTH, DECAY_INNER), MODEL_WIDTH ** -0.5, 0.09375),
        "fading_raise_matrix": scatter_about(splits[9], (DECAY_INNER, MODEL_WIDTH), 0.15, 1.0, ((1, 8),)),
        "diagonal_boost": scatter_about(splits[10], (ATTENTION_GROUPS, GROUP_DIMENSION), 0.5, 3.0, ((0, 8),), jnp.float32),
        "acceptor_matrix": scatter_about(splits[11], (MODEL_WIDTH, MODEL_WIDTH), MODEL_WIDTH ** -0.5, 0.09375, ((0, 4), (1, 8))),
        "lookup_matrix": scatter_about(splits[12], (MODEL_WIDTH, MODEL_WIDTH), MODEL_WIDTH ** -0.5, 0.09375, ((0, 4), (1, 8))),
        "payload_matrix": scatter_about(splits[13], (MODEL_WIDTH, MODEL_WIDTH), MODEL_WIDTH ** -0.5, 0.09375, ((0, 4), (1, 8))),
        "gating_matrix": scatter_about(splits[14], (MODEL_WIDTH, MODEL_WIDTH), MODEL_WIDTH ** -0.5, 0.09375, ((0, 4), (1, 8))),
        "emission_matrix": scatter_about(splits[15], (MODEL_WIDTH, MODEL_WIDTH), MODEL_WIDTH ** -0.5, 0.09375, ((0, 8), (1, 4))),
        "groupwise_scaling_factor": jnp.clip(1.0 + 0.18 * jax.random.normal(splits[16], (MODEL_WIDTH,), jnp.float32), 0.1, 1.9),
        "groupwise_scaling_offset": scatter_about(splits[17], (MODEL_WIDTH,), 0.5, 3.0, ((0, 8),), jnp.float32),
        "usable_guess_amount": draw_usable_guess_amount(jax.random.fold_in(splits[21], 71), 0),
        "approved_guesses": draw_approved_guesses(jax.random.fold_in(splits[21], 71), 0),
        "destination_slot": draw_destination_slot(jax.random.fold_in(splits[21], 71), 0),
    }


norm_eps = 0.00064

def token_mixes(guess_vectors, edges, lag_blend_factor, constant_lag_blends, blending_lower_matrix, blending_raise_matrix):
    previous = jnp.concatenate([edges[:, None, :], guess_vectors[:, :-1, :]], axis=1)
    width = guess_vectors.shape[-1]
    current_input = guess_vectors.reshape(-1, width).astype(jnp.float32)
    shift_difference = previous.reshape(-1, width).astype(jnp.float32) - current_input
    shift_blended = (current_input + shift_difference * lag_blend_factor).astype(jnp.bfloat16)
    mixing_inner_all = jnp.tanh(jnp.dot(shift_blended, blending_lower_matrix, preferred_element_type=jnp.float32)).astype(jnp.bfloat16)
    mixing_inner_width = blending_raise_matrix.shape[1]
    shift_mixed_rows = []
    for mix_component in range(5):
        mixing_inner_part = jnp.dot(mixing_inner_all[:, mix_component * mixing_inner_width:(mix_component + 1) * mixing_inner_width], blending_raise_matrix[mix_component], preferred_element_type=jnp.float32)
        shift_mixed_rows.append((current_input + shift_difference * (constant_lag_blends[mix_component] + mixing_inner_part)).astype(jnp.bfloat16))
    return shift_mixed_rows

def iteration_results(acceptor_vectors, lookup_vectors, payload_vectors, logarithmic_fading_entries, diagonal_boost, starting_memory, approved_guesses):
    decay = jnp.exp(logarithmic_fading_entries)
    picked_start = jnp.where((approved_guesses == 0)[:, None, None, None], starting_memory, jnp.zeros_like(starting_memory))

    def advance(carry, inputs):
        memory_matrix, picked = carry
        position, present_acceptor_vector, present_lookup_vector, present_payload_vector, decay_now = inputs
        diagonal_boost_contribution = lax.optimization_barrier(jnp.sum(present_acceptor_vector * diagonal_boost * present_lookup_vector, axis=-1, keepdims=True)) * present_payload_vector
        layer_result = jnp.einsum('ges,gesm->gem', present_acceptor_vector, memory_matrix, precision=lax.Precision.HIGHEST) + diagonal_boost_contribution
        memory_matrix = decay_now[..., None] * memory_matrix + present_lookup_vector[..., None] * present_payload_vector[..., None, :]
        picked = jnp.where((approved_guesses == position + 1)[:, None, None, None], memory_matrix, picked)
        return ((memory_matrix, picked), layer_result)
    steps_in = (jnp.arange(acceptor_vectors.shape[1], dtype=jnp.int32), jnp.swapaxes(acceptor_vectors, 0, 1), jnp.swapaxes(lookup_vectors, 0, 1), jnp.swapaxes(payload_vectors, 0, 1), jnp.swapaxes(decay, 0, 1))
    (final_state, picked), outputs = lax.scan(advance, (starting_memory, picked_start), steps_in)
    return (jnp.swapaxes(outputs, 0, 1), picked)

def gated_norm(outputs, gate_raw, gain, bias):
    centre = lax.optimization_barrier(jnp.mean(outputs, axis=-1, keepdims=True))
    spread = outputs - centre
    variance = lax.optimization_barrier(jnp.mean(spread * spread, axis=-1, keepdims=True))
    normed = (spread * lax.rsqrt(variance + norm_eps)).reshape(outputs.shape[0], -1)
    return ((normed * gain + bias) * jax.nn.silu(gate_raw)).astype(jnp.bfloat16)

def reference(guess_vectors, preceding_symbol_vector, earlier_memory_matrix, lag_blend_factor, constant_lag_blends, blending_lower_matrix, blending_raise_matrix, constant_fading, fading_lower_matrix, fading_raise_matrix, diagonal_boost, acceptor_matrix, lookup_matrix, payload_matrix, gating_matrix, emission_matrix, groupwise_scaling_factor, groupwise_scaling_offset, usable_guess_amount, approved_guesses, destination_slot):
    token_count = REQ * DRAFT
    shift_mixed_rows = token_mixes(guess_vectors, preceding_symbol_vector, lag_blend_factor, constant_lag_blends, blending_lower_matrix, blending_raise_matrix)
    acceptor_vectors = jnp.dot(shift_mixed_rows[3], acceptor_matrix, preferred_element_type=jnp.float32)
    lookup_vectors = jnp.dot(shift_mixed_rows[1], lookup_matrix, preferred_element_type=jnp.float32)
    payload_vectors = jnp.dot(shift_mixed_rows[2], payload_matrix, preferred_element_type=jnp.float32)
    gate_raw = jnp.dot(shift_mixed_rows[4], gating_matrix, preferred_element_type=jnp.float32)
    decay_inner_rows = jnp.tanh(jnp.dot(shift_mixed_rows[0], fading_lower_matrix, preferred_element_type=jnp.float32)).astype(jnp.bfloat16)
    logarithmic_fading_entries = -jnp.exp(constant_fading + jnp.dot(decay_inner_rows, fading_raise_matrix, preferred_element_type=jnp.float32))
    blocks = REQ // REQ_ROW

    def to_heads(values):
        return values.reshape(blocks, REQ_ROW, DRAFT, ATTENTION_GROUPS, GROUP_DIMENSION)

    def run_block(inputs):
        acceptor_tile, lookup_vectors_tile, payload_vectors_tile, fading_entries_tile, memory_entries_tile, retained_memory_tile = inputs
        return iteration_results(acceptor_tile, lookup_vectors_tile, payload_vectors_tile, fading_entries_tile, diagonal_boost, memory_entries_tile, retained_memory_tile)
    outputs, picked = lax.map(run_block, (to_heads(acceptor_vectors), to_heads(lookup_vectors), to_heads(payload_vectors), to_heads(logarithmic_fading_entries), earlier_memory_matrix.reshape(blocks, REQ_ROW, ATTENTION_GROUPS, GROUP_DIMENSION, GROUP_DIMENSION), approved_guesses.reshape(blocks, REQ_ROW)))
    outputs = outputs.reshape(token_count, ATTENTION_GROUPS, GROUP_DIMENSION)
    picked = picked.reshape(REQ, ATTENTION_GROUPS, GROUP_DIMENSION, GROUP_DIMENSION)
    hidden = gated_norm(outputs, gate_raw, groupwise_scaling_factor, groupwise_scaling_offset)
    group_width = MODEL_WIDTH // N_MP
    grouped = jnp.swapaxes(hidden.reshape(token_count, N_MP, group_width), 0, 1)
    out_rows = emission_matrix.reshape(N_MP, group_width, MODEL_WIDTH)

    def add_group(running, pieces):
        hidden_group, rows_group = pieces
        rounded = lax.optimization_barrier(jnp.dot(hidden_group, rows_group, preferred_element_type=jnp.float32).astype(jnp.bfloat16))
        return (running + rounded.astype(jnp.float32), None)
    attended, unused = lax.scan(add_group, jnp.zeros((token_count, MODEL_WIDTH), jnp.float32), (grouped, out_rows))
    valid_mask = jnp.arange(DRAFT, dtype=jnp.int32)[None, :] < usable_guess_amount[:, None]
    layer_out = (guess_vectors.astype(jnp.float32) + jnp.where(valid_mask[..., None], attended.reshape(REQ, DRAFT, MODEL_WIDTH), jnp.zeros((), jnp.float32))).astype(jnp.bfloat16)
    edge_rows = jnp.concatenate([preceding_symbol_vector[:, None, :], guess_vectors], axis=1)
    chosen = jnp.take_along_axis(edge_rows, approved_guesses.astype(jnp.int32)[:, None, None], axis=1)[:, 0]
    next_state = jnp.zeros_like(picked).at[destination_slot].set(picked)
    next_edge = jnp.zeros_like(chosen).at[destination_slot].set(chosen)
    return (layer_out, next_state, next_edge)
```

```python
import jax
import jax.numpy as jnp
from jax import lax
from jax.sharding import PartitionSpec as P

GROUP_DIMENSION = 64


norm_eps = 0.00064


def shift(guess_vectors, edges):
    previous = jnp.concatenate([edges[..., None, :], guess_vectors[..., :-1, :]], axis=-2)
    current_input = guess_vectors.astype(jnp.float32)
    return current_input, previous.astype(jnp.float32) - current_input


def dot32(left, right):
    return jnp.dot(left, right, preferred_element_type=jnp.float32)


def mix(current_input, shift_difference, constant, inner, raise_matrix):
    return (current_input + shift_difference * (constant + dot32(inner, raise_matrix))).astype(
        jnp.bfloat16
    )


def wkv_blocks(
    acceptor_vectors,
    lookup_vectors,
    payload_vectors,
    logarithmic_fading_entries,
    diagonal_boost,
    starting_memory,
    approved_guesses,
):
    draft = acceptor_vectors.shape[1]
    cumulative = jnp.cumsum(logarithmic_fading_entries, axis=1)
    starts = jnp.concatenate(
        [jnp.zeros_like(logarithmic_fading_entries[:, :1]), cumulative], axis=1
    )
    before = starts[:, :draft]
    from_start = jnp.einsum(
        "bthi,bhij->bthj",
        acceptor_vectors * jnp.exp(before),
        starting_memory,
        precision=lax.Precision.HIGHEST,
    )
    later = jnp.arange(draft)[:, None] > jnp.arange(draft)[None, :]
    exponent = before[:, :, None] - cumulative[:, None, :]
    exponent = jnp.where(later[None, :, :, None, None], exponent, -1e30)
    scores = jnp.sum(
        acceptor_vectors[:, :, None] * lookup_vectors[:, None, :] * jnp.exp(exponent), axis=-1
    )
    inner = jnp.einsum("btsh,bshj->bthj", scores, payload_vectors, precision=lax.Precision.HIGHEST)
    diagonal_boost_contribution = (
        jnp.sum(acceptor_vectors * diagonal_boost * lookup_vectors, axis=-1, keepdims=True)
        * payload_vectors
    )
    outputs = from_start + inner + diagonal_boost_contribution
    at_accept = jnp.take_along_axis(starts, approved_guesses[:, None, None, None], axis=1)[:, 0]
    used = jnp.arange(draft)[None, :] < approved_guesses[:, None]
    coef_exp = jnp.where(used[:, :, None, None], at_accept[:, None] - cumulative, -1e30)
    weighted = jnp.exp(coef_exp) * lookup_vectors
    picked = jnp.exp(at_accept)[..., None] * starting_memory + jnp.einsum(
        "bshi,bshj->bhij", weighted, payload_vectors, precision=lax.Precision.HIGHEST
    )
    return (outputs, picked)


def gated_norm(outputs, gate_raw, gain, bias):
    centre = jnp.mean(outputs, axis=-1, keepdims=True)
    spread = outputs - centre
    variance = jnp.mean(spread * spread, axis=-1, keepdims=True)
    normed = (spread * lax.rsqrt(variance + norm_eps)).reshape(outputs.shape[0], -1)
    return ((normed * gain + bias) * jax.nn.silu(gate_raw)).astype(jnp.bfloat16)


def on_device(
    guess_vectors,
    preceding_symbol_vector,
    earlier_memory_matrix,
    lag_blend_factor,
    constant_lag_blends,
    blending_lower_matrix,
    blending_raise_matrix,
    constant_fading,
    fading_lower_matrix,
    fading_raise_matrix,
    diagonal_boost,
    acceptor_matrix,
    lookup_matrix,
    payload_matrix,
    gating_matrix,
    emission_matrix,
    groupwise_scaling_factor,
    groupwise_scaling_offset,
    usable_guess_amount,
    approved_guesses,
    destination_slot,
):
    own_reqs, draft, width = guess_vectors.shape
    group_count = lax.axis_size("mp")
    row_groups = lax.axis_size("dp")
    row_reqs = own_reqs * group_count
    row_index = lax.axis_index("dp")
    group_index = lax.axis_index("mp")
    local_width = acceptor_matrix.shape[1]
    local_heads = local_width // GROUP_DIMENSION
    inner_width = blending_raise_matrix.shape[1]
    decay_width = fading_lower_matrix.shape[1]
    own_tokens = own_reqs * draft
    col_width = width // row_groups
    own_current, own_difference = shift(guess_vectors, preceding_symbol_vector)
    own_current = own_current.reshape(own_tokens, width)
    own_difference = own_difference.reshape(own_tokens, width)
    blended = (own_current + own_difference * lag_blend_factor).astype(jnp.bfloat16)
    own_inner = jnp.tanh(dot32(blended, blending_lower_matrix)).astype(jnp.bfloat16)
    own_decay_mix = mix(
        own_current,
        own_difference,
        constant_lag_blends[0],
        own_inner[:, :inner_width],
        blending_raise_matrix[0],
    )
    own_decay_inner = jnp.tanh(dot32(own_decay_mix, fading_lower_matrix)).astype(jnp.bfloat16)
    own_narrow = jnp.concatenate([own_inner, own_decay_inner], axis=1)
    narrow_width = own_narrow.shape[1]
    narrow_rows = own_tokens * narrow_width // col_width

    def by_columns(rows):
        return rows.reshape(-1, row_groups, col_width).transpose(1, 0, 2)

    packed = jnp.concatenate(
        [
            by_columns(guess_vectors.reshape(own_tokens, width)),
            by_columns(preceding_symbol_vector),
            jnp.broadcast_to(
                own_narrow.reshape(1, narrow_rows, col_width),
                (row_groups, narrow_rows, col_width),
            ),
        ],
        axis=1,
    )
    packed = lax.all_to_all(packed, "dp", split_axis=0, concat_axis=0, tiled=True)
    packed = lax.all_gather(packed, "mp", axis=0, tiled=False)
    packed = packed.transpose(1, 0, 2, 3)
    tokens = packed[:, :, :own_tokens].reshape(
        row_groups, group_count, own_reqs, draft, col_width
    )
    edges = packed[:, :, own_tokens : own_tokens + own_reqs]
    narrow = packed[:, :, own_tokens + own_reqs :].reshape(
        row_groups, group_count * own_tokens, narrow_width
    )
    all_tokens = row_groups * group_count * own_tokens
    current, difference = shift(tokens, edges)
    current = current.reshape(all_tokens, col_width)
    difference = difference.reshape(all_tokens, col_width)
    inner_all = narrow.reshape(all_tokens, narrow_width)
    col_start = row_index * col_width
    constants = lax.dynamic_slice_in_dim(constant_lag_blends, col_start, col_width, 1)
    raises = lax.dynamic_slice_in_dim(blending_raise_matrix, col_start, col_width, 2)

    def partial(component, matrix):
        mixed = mix(
            current,
            difference,
            constants[component],
            inner_all[:, component * inner_width : (component + 1) * inner_width],
            raises[component],
        )
        return dot32(mixed, matrix).astype(jnp.bfloat16)

    def summed(values):
        return lax.psum_scatter(values, "dp", scatter_dimension=0, tiled=True).astype(jnp.float32)

    token_rows = row_reqs * draft
    triple = summed(
        jnp.concatenate(
            [
                partial(3, acceptor_matrix),
                partial(1, lookup_matrix),
                partial(2, payload_matrix),
            ],
            axis=1,
        )
    )
    acceptor_vectors, lookup_vectors, payload_vectors = jnp.split(triple, 3, axis=1)
    gate_raw = summed(partial(4, gating_matrix))
    row_narrow = lax.dynamic_index_in_dim(narrow, row_index, 0, keepdims=False)
    decay_inner_rows = row_narrow[:, narrow_width - decay_width :]
    logarithmic_fading_entries = -jnp.exp(
        constant_fading + dot32(decay_inner_rows, fading_raise_matrix)
    )

    def to_heads(values):
        return values.reshape(row_reqs, draft, local_heads, GROUP_DIMENSION)

    row_accepted = lax.dynamic_slice_in_dim(approved_guesses, row_index * row_reqs, row_reqs)
    outputs, picked = wkv_blocks(
        to_heads(acceptor_vectors),
        to_heads(lookup_vectors),
        to_heads(payload_vectors),
        to_heads(logarithmic_fading_entries),
        diagonal_boost,
        earlier_memory_matrix,
        row_accepted,
    )
    hidden = gated_norm(
        outputs.reshape(token_rows, local_heads, GROUP_DIMENSION),
        gate_raw,
        groupwise_scaling_factor,
        groupwise_scaling_offset,
    )
    out_cols = lax.all_gather(emission_matrix, "dp", axis=1, tiled=True)
    attended = lax.psum_scatter(
        jnp.dot(hidden, out_cols, preferred_element_type=jnp.float32).astype(jnp.bfloat16),
        "mp",
        scatter_dimension=0,
        tiled=True,
    ).astype(jnp.float32)
    own_start = (row_index * group_count + group_index) * own_reqs
    own_lengths = lax.dynamic_slice_in_dim(usable_guess_amount, own_start, own_reqs)
    valid_mask = jnp.arange(draft, dtype=jnp.int32)[None, :] < own_lengths[:, None]
    layer_out = (
        guess_vectors.astype(jnp.float32)
        + jnp.where(
            valid_mask[..., None],
            attended.reshape(own_reqs, draft, width),
            jnp.zeros((), jnp.float32),
        )
    ).astype(jnp.bfloat16)
    own_accepted = lax.dynamic_slice_in_dim(approved_guesses, own_start, own_reqs)
    edge_rows = jnp.concatenate([preceding_symbol_vector[:, None, :], guess_vectors], axis=1)
    own_chosen = jnp.take_along_axis(edge_rows, own_accepted[:, None, None], axis=1)[:, 0]
    chosen = lax.all_gather(own_chosen, ("dp", "mp"), axis=0, tiled=True)
    chosen_cols = lax.dynamic_slice_in_dim(chosen, group_index * local_width, local_width, 1)
    capacity = 2 * row_reqs // row_groups
    target_rows = (destination_slot // row_reqs).reshape(row_groups, row_reqs)
    onehot = (
        target_rows[:, :, None] == jnp.arange(row_groups, dtype=jnp.int32)[None, None, :]
    ).astype(jnp.int32)
    earlier = jnp.cumsum(onehot, axis=1) - onehot
    ranks = jnp.sum(earlier * onehot, axis=-1)
    my_targets = lax.dynamic_index_in_dim(target_rows, row_index, 0, keepdims=False)
    my_ranks = lax.dynamic_index_in_dim(ranks, row_index, 0, keepdims=False)
    selected = (
        my_targets[:, None, None] == jnp.arange(row_groups, dtype=jnp.int32)[None, :, None]
    ) & (my_ranks[:, None, None] == jnp.arange(capacity, dtype=jnp.int32)[None, None, :])
    source_index = jnp.sum(
        selected.astype(jnp.int32) * jnp.arange(row_reqs, dtype=jnp.int32)[:, None, None], axis=0
    )
    send_state = picked.astype(jnp.bfloat16)[source_index]
    recv_state = lax.all_to_all(send_state, "dp", split_axis=0, concat_axis=0, tiled=True)
    wanted = row_index * row_reqs + jnp.arange(row_reqs, dtype=jnp.int32)
    total_reqs = destination_slot.shape[0]
    matches = (destination_slot[None, :] == wanted[:, None]).astype(jnp.int32)
    which = jnp.sum(matches * jnp.arange(total_reqs, dtype=jnp.int32)[None, :], axis=1)
    flat_index = which // row_reqs * capacity + ranks.reshape(-1)[which]
    next_state = recv_state.reshape(
        row_groups * capacity, local_heads, GROUP_DIMENSION, GROUP_DIMENSION
    )[flat_index].astype(jnp.float32)
    next_edge = chosen_cols[which]
    return (layer_out, next_state, next_edge)


def solution(mesh):
    in_specs = (
        P(("dp", "mp"), None, None),
        P(("dp", "mp"), None),
        P("dp", "mp", None, None),
        P(),
        P(),
        P(),
        P(),
        P("mp"),
        P(),
        P(None, "mp"),
        P("mp", None),
        P("dp", "mp"),
        P("dp", "mp"),
        P("dp", "mp"),
        P("dp", "mp"),
        P("mp", "dp"),
        P("mp"),
        P("mp"),
        P(),
        P(),
        P(),
    )
    out_specs = (P(("dp", "mp"), None, None), P("dp", "mp", None, None), P("dp", "mp"))
    return jax.shard_map(
        on_device, mesh=mesh, in_specs=in_specs, out_specs=out_specs, check_vma=False
    )
```

```python
import jax
import jax.numpy as jnp
from jax import lax
from jax.sharding import PartitionSpec as P

GROUP_DIMENSION = 64


norm_eps = 0.00064


def shift(guess_vectors, edges):
    previous = jnp.concatenate([edges[..., None, :], guess_vectors[..., :-1, :]], axis=-2)
    current_input = guess_vectors.astype(jnp.float32)
    return current_input, previous.astype(jnp.float32) - current_input


def dot32(left, right):
    return jnp.dot(left, right, preferred_element_type=jnp.float32)


def mix(current_input, shift_difference, constant, inner, raise_matrix):
    return (current_input + shift_difference * (constant + dot32(inner, raise_matrix))).astype(
        jnp.bfloat16
    )


def wkv_blocks(
    acceptor_vectors,
    lookup_vectors,
    payload_vectors,
    logarithmic_fading_entries,
    diagonal_boost,
    starting_memory,
    approved_guesses,
):
    draft = acceptor_vectors.shape[1]
    cumulative = jnp.cumsum(logarithmic_fading_entries, axis=1)
    starts = jnp.concatenate(
        [jnp.zeros_like(logarithmic_fading_entries[:, :1]), cumulative], axis=1
    )
    before = starts[:, :draft]
    from_start = jnp.einsum(
        "bthi,bhij->bthj",
        acceptor_vectors * jnp.exp(before),
        starting_memory,
        precision=lax.Precision.HIGHEST,
    )
    later = jnp.arange(draft)[:, None] > jnp.arange(draft)[None, :]
    exponent = before[:, :, None] - cumulative[:, None, :]
    exponent = jnp.where(later[None, :, :, None, None], exponent, -1e30)
    scores = jnp.sum(
        acceptor_vectors[:, :, None] * lookup_vectors[:, None, :] * jnp.exp(exponent), axis=-1
    )
    inner = jnp.einsum("btsh,bshj->bthj", scores, payload_vectors, precision=lax.Precision.HIGHEST)
    diagonal_boost_contribution = (
        jnp.sum(acceptor_vectors * diagonal_boost * lookup_vectors, axis=-1, keepdims=True)
        * payload_vectors
    )
    outputs = from_start + inner + diagonal_boost_contribution
    at_accept = jnp.take_along_axis(starts, approved_guesses[:, None, None, None], axis=1)[:, 0]
    used = jnp.arange(draft)[None, :] < approved_guesses[:, None]
    coef_exp = jnp.where(used[:, :, None, None], at_accept[:, None] - cumulative, -1e30)
    weighted = jnp.exp(coef_exp) * lookup_vectors
    picked = jnp.exp(at_accept)[..., None] * starting_memory + jnp.einsum(
        "bshi,bshj->bhij", weighted, payload_vectors, precision=lax.Precision.HIGHEST
    )
    return (outputs, picked)


def gated_norm(outputs, gate_raw, gain, bias):
    centre = jnp.mean(outputs, axis=-1, keepdims=True)
    spread = outputs - centre
    variance = jnp.mean(spread * spread, axis=-1, keepdims=True)
    normed = (spread * lax.rsqrt(variance + norm_eps)).reshape(outputs.shape[0], -1)
    return ((normed * gain + bias) * jax.nn.silu(gate_raw)).astype(jnp.bfloat16)


def on_device(
    guess_vectors,
    preceding_symbol_vector,
    earlier_memory_matrix,
    lag_blend_factor,
    constant_lag_blends,
    blending_lower_matrix,
    blending_raise_matrix,
    constant_fading,
    fading_lower_matrix,
    fading_raise_matrix,
    diagonal_boost,
    acceptor_matrix,
    lookup_matrix,
    payload_matrix,
    gating_matrix,
    emission_matrix,
    groupwise_scaling_factor,
    groupwise_scaling_offset,
    usable_guess_amount,
    approved_guesses,
    destination_slot,
):
    own_reqs, draft, width = guess_vectors.shape
    group_count = lax.axis_size("mp")
    row_groups = lax.axis_size("dp")
    row_reqs = own_reqs * group_count
    row_index = lax.axis_index("dp")
    group_index = lax.axis_index("mp")
    local_width = acceptor_matrix.shape[1]
    local_heads = local_width // GROUP_DIMENSION
    inner_width = blending_raise_matrix.shape[1]
    decay_width = fading_lower_matrix.shape[1]
    own_tokens = own_reqs * draft
    col_width = width // row_groups
    own_current, own_difference = shift(guess_vectors, preceding_symbol_vector)
    own_current = own_current.reshape(own_tokens, width)
    own_difference = own_difference.reshape(own_tokens, width)
    blended = (own_current + own_difference * lag_blend_factor).astype(jnp.bfloat16)
    own_inner = jnp.tanh(dot32(blended, blending_lower_matrix)).astype(jnp.bfloat16)
    own_decay_mix = mix(
        own_current,
        own_difference,
        constant_lag_blends[0],
        own_inner[:, :inner_width],
        blending_raise_matrix[0],
    )
    own_decay_inner = jnp.tanh(dot32(own_decay_mix, fading_lower_matrix)).astype(jnp.bfloat16)
    own_narrow = jnp.concatenate([own_inner, own_decay_inner], axis=1)
    narrow_width = own_narrow.shape[1]
    narrow_rows = own_tokens * narrow_width // col_width

    def by_columns(rows):
        return rows.reshape(-1, row_groups, col_width).transpose(1, 0, 2)

    packed = jnp.concatenate(
        [
            by_columns(guess_vectors.reshape(own_tokens, width)),
            by_columns(preceding_symbol_vector),
            jnp.broadcast_to(
                own_narrow.reshape(1, narrow_rows, col_width),
                (row_groups, narrow_rows, col_width),
            ),
        ],
        axis=1,
    )
    packed = lax.all_to_all(packed, "dp", split_axis=0, concat_axis=0, tiled=True)
    packed = lax.all_gather(packed, "mp", axis=0, tiled=False)
    packed = packed.transpose(1, 0, 2, 3)
    tokens = packed[:, :, :own_tokens].reshape(
        row_groups, group_count, own_reqs, draft, col_width
    )
    edges = packed[:, :, own_tokens : own_tokens + own_reqs]
    narrow = packed[:, :, own_tokens + own_reqs :].reshape(
        row_groups, group_count * own_tokens, narrow_width
    )
    all_tokens = row_groups * group_count * own_tokens
    current, difference = shift(tokens, edges)
    current = current.reshape(all_tokens, col_width)
    difference = difference.reshape(all_tokens, col_width)
    inner_all = narrow.reshape(all_tokens, narrow_width)
    col_start = row_index * col_width
    constants = lax.dynamic_slice_in_dim(constant_lag_blends, col_start, col_width, 1)
    raises = lax.dynamic_slice_in_dim(blending_raise_matrix, col_start, col_width, 2)

    def partial(component, matrix):
        mixed = mix(
            current,
            difference,
            constants[component],
            inner_all[:, component * inner_width : (component + 1) * inner_width],
            raises[component],
        )
        return dot32(mixed, matrix).astype(jnp.bfloat16)

    def summed(values):
        return lax.psum_scatter(values, "dp", scatter_dimension=0, tiled=True).astype(jnp.float32)

    token_rows = row_reqs * draft
    triple = summed(
        jnp.concatenate(
            [
                partial(3, acceptor_matrix),
                partial(1, lookup_matrix),
                partial(2, payload_matrix),
            ],
            axis=1,
        )
    )
    acceptor_vectors, lookup_vectors, payload_vectors = jnp.split(triple, 3, axis=1)
    gate_summed = lax.psum_scatter(
        partial(4, gating_matrix), "dp", scatter_dimension=0, tiled=True
    )
    gate_raw = gate_summed.astype(jnp.float32)
    row_narrow = lax.dynamic_index_in_dim(narrow, row_index, 0, keepdims=False)
    decay_inner_rows = row_narrow[:, narrow_width - decay_width :]
    logarithmic_fading_entries = -jnp.exp(
        constant_fading + dot32(decay_inner_rows, fading_raise_matrix)
    )

    def to_heads(values):
        return values.reshape(row_reqs, draft, local_heads, GROUP_DIMENSION)

    row_accepted = lax.dynamic_slice_in_dim(approved_guesses, row_index * row_reqs, row_reqs)
    outputs, picked = wkv_blocks(
        to_heads(acceptor_vectors),
        to_heads(lookup_vectors),
        to_heads(payload_vectors),
        to_heads(logarithmic_fading_entries),
        diagonal_boost,
        earlier_memory_matrix,
        row_accepted,
    )
    hidden = gated_norm(
        outputs.reshape(token_rows, local_heads, GROUP_DIMENSION),
        gate_raw,
        groupwise_scaling_factor,
        groupwise_scaling_offset,
    )
    emission_matrix, gate_summed = lax.optimization_barrier((emission_matrix, gate_summed))
    out_cols = lax.all_gather(emission_matrix, "dp", axis=1, tiled=True)
    attended = lax.psum_scatter(
        jnp.dot(hidden, out_cols, preferred_element_type=jnp.float32).astype(jnp.bfloat16),
        "mp",
        scatter_dimension=0,
        tiled=True,
    ).astype(jnp.float32)
    own_start = (row_index * group_count + group_index) * own_reqs
    own_lengths = lax.dynamic_slice_in_dim(usable_guess_amount, own_start, own_reqs)
    valid_mask = jnp.arange(draft, dtype=jnp.int32)[None, :] < own_lengths[:, None]
    layer_out = (
        guess_vectors.astype(jnp.float32)
        + jnp.where(
            valid_mask[..., None],
            attended.reshape(own_reqs, draft, width),
            jnp.zeros((), jnp.float32),
        )
    ).astype(jnp.bfloat16)
    own_accepted = lax.dynamic_slice_in_dim(approved_guesses, own_start, own_reqs)
    edge_rows = jnp.concatenate([preceding_symbol_vector[:, None, :], guess_vectors], axis=1)
    own_chosen = jnp.take_along_axis(edge_rows, own_accepted[:, None, None], axis=1)[:, 0]
    row_chosen = lax.all_gather(own_chosen, "mp", axis=0, tiled=True)
    chosen_cols = lax.all_gather(
        lax.dynamic_slice_in_dim(row_chosen, group_index * local_width, local_width, 1),
        "dp",
        axis=0,
        tiled=True,
    )
    capacity = 2 * row_reqs // row_groups
    target_rows = (destination_slot // row_reqs).reshape(row_groups, row_reqs)
    onehot = (
        target_rows[:, :, None] == jnp.arange(row_groups, dtype=jnp.int32)[None, None, :]
    ).astype(jnp.int32)
    earlier = jnp.cumsum(onehot, axis=1) - onehot
    ranks = jnp.sum(earlier * onehot, axis=-1)
    my_targets = lax.dynamic_index_in_dim(target_rows, row_index, 0, keepdims=False)
    my_ranks = lax.dynamic_index_in_dim(ranks, row_index, 0, keepdims=False)
    selected = (
        my_targets[:, None, None] == jnp.arange(row_groups, dtype=jnp.int32)[None, :, None]
    ) & (my_ranks[:, None, None] == jnp.arange(capacity, dtype=jnp.int32)[None, None, :])
    source_index = jnp.sum(
        selected.astype(jnp.int32) * jnp.arange(row_reqs, dtype=jnp.int32)[:, None, None], axis=0
    )
    send_state = picked.astype(jnp.bfloat16)[source_index]
    recv_state = lax.all_to_all(send_state, "dp", split_axis=0, concat_axis=0, tiled=True)
    wanted = row_index * row_reqs + jnp.arange(row_reqs, dtype=jnp.int32)
    total_reqs = destination_slot.shape[0]
    matches = (destination_slot[None, :] == wanted[:, None]).astype(jnp.int32)
    which = jnp.sum(matches * jnp.arange(total_reqs, dtype=jnp.int32)[None, :], axis=1)
    flat_index = which // row_reqs * capacity + ranks.reshape(-1)[which]
    next_state = recv_state.reshape(
        row_groups * capacity, local_heads, GROUP_DIMENSION, GROUP_DIMENSION
    )[flat_index].astype(jnp.float32)
    next_edge = chosen_cols[which]
    return (layer_out, next_state, next_edge)


def solution(mesh):
    in_specs = (
        P(("dp", "mp"), None, None),
        P(("dp", "mp"), None),
        P("dp", "mp", None, None),
        P(),
        P(),
        P(),
        P(),
        P("mp"),
        P(),
        P(None, "mp"),
        P("mp", None),
        P("dp", "mp"),
        P("dp", "mp"),
        P("dp", "mp"),
        P("dp", "mp"),
        P("mp", "dp"),
        P("mp"),
        P("mp"),
        P(),
        P(),
        P(),
    )
    out_specs = (P(("dp", "mp"), None, None), P("dp", "mp", None, None), P("dp", "mp"))
    return jax.shard_map(
        on_device, mesh=mesh, in_specs=in_specs, out_specs=out_specs, check_vma=False
    )
```

```python
import jax
import jax.numpy as jnp
from jax import lax
from jax.sharding import PartitionSpec as P

GROUP_DIMENSION = 64


norm_eps = 0.00064


def shift(guess_vectors, edges):
    previous = jnp.concatenate([edges[..., None, :], guess_vectors[..., :-1, :]], axis=-2)
    current_input = guess_vectors.astype(jnp.float32)
    return current_input, previous.astype(jnp.float32) - current_input


def dot32(left, right):
    return jnp.dot(left, right, preferred_element_type=jnp.float32)


def mix(current_input, shift_difference, constant, inner, raise_matrix):
    return (current_input + shift_difference * (constant + dot32(inner, raise_matrix))).astype(
        jnp.bfloat16
    )


def fading_sums(logarithmic_fading_entries):
    cumulative = jnp.cumsum(logarithmic_fading_entries, axis=1)
    starts = jnp.concatenate(
        [jnp.zeros_like(logarithmic_fading_entries[:, :1]), cumulative], axis=1
    )
    return cumulative, starts


def picked_states(
    lookup_vectors, payload_vectors, cumulative, starts, starting_memory, approved_guesses
):
    draft = lookup_vectors.shape[1]
    at_accept = jnp.take_along_axis(starts, approved_guesses[:, None, None, None], axis=1)[:, 0]
    used = jnp.arange(draft)[None, :] < approved_guesses[:, None]
    coef_exp = jnp.where(used[:, :, None, None], at_accept[:, None] - cumulative, -1e30)
    weighted = jnp.exp(coef_exp) * lookup_vectors
    return jnp.exp(at_accept)[..., None] * starting_memory + jnp.einsum(
        "bshi,bshj->bhij", weighted, payload_vectors, precision=lax.Precision.HIGHEST
    )


def wkv_blocks(
    acceptor_vectors,
    lookup_vectors,
    payload_vectors,
    cumulative,
    starts,
    diagonal_boost,
    starting_memory,
):
    draft = acceptor_vectors.shape[1]
    before = starts[:, :draft]
    from_start = jnp.einsum(
        "bthi,bhij->bthj",
        acceptor_vectors * jnp.exp(before),
        starting_memory,
        precision=lax.Precision.HIGHEST,
    )
    later = jnp.arange(draft)[:, None] > jnp.arange(draft)[None, :]
    exponent = before[:, :, None] - cumulative[:, None, :]
    exponent = jnp.where(later[None, :, :, None, None], exponent, -1e30)
    scores = jnp.sum(
        acceptor_vectors[:, :, None] * lookup_vectors[:, None, :] * jnp.exp(exponent), axis=-1
    )
    inner = jnp.einsum("btsh,bshj->bthj", scores, payload_vectors, precision=lax.Precision.HIGHEST)
    diagonal_boost_contribution = (
        jnp.sum(acceptor_vectors * diagonal_boost * lookup_vectors, axis=-1, keepdims=True)
        * payload_vectors
    )
    return from_start + inner + diagonal_boost_contribution


def gated_norm(outputs, gate_raw, gain, bias):
    centre = jnp.mean(outputs, axis=-1, keepdims=True)
    spread = outputs - centre
    variance = jnp.mean(spread * spread, axis=-1, keepdims=True)
    normed = (spread * lax.rsqrt(variance + norm_eps)).reshape(outputs.shape[0], -1)
    return ((normed * gain + bias) * jax.nn.silu(gate_raw)).astype(jnp.bfloat16)


def on_device(
    guess_vectors,
    preceding_symbol_vector,
    earlier_memory_matrix,
    lag_blend_factor,
    constant_lag_blends,
    blending_lower_matrix,
    blending_raise_matrix,
    constant_fading,
    fading_lower_matrix,
    fading_raise_matrix,
    diagonal_boost,
    acceptor_matrix,
    lookup_matrix,
    payload_matrix,
    gating_matrix,
    emission_matrix,
    groupwise_scaling_factor,
    groupwise_scaling_offset,
    usable_guess_amount,
    approved_guesses,
    destination_slot,
):
    own_reqs, draft, width = guess_vectors.shape
    group_count = lax.axis_size("mp")
    row_groups = lax.axis_size("dp")
    row_reqs = own_reqs * group_count
    row_index = lax.axis_index("dp")
    group_index = lax.axis_index("mp")
    local_width = acceptor_matrix.shape[1]
    local_heads = local_width // GROUP_DIMENSION
    inner_width = blending_raise_matrix.shape[1]
    decay_width = fading_lower_matrix.shape[1]
    own_tokens = own_reqs * draft
    col_width = width // row_groups
    own_current, own_difference = shift(guess_vectors, preceding_symbol_vector)
    own_current = own_current.reshape(own_tokens, width)
    own_difference = own_difference.reshape(own_tokens, width)
    blended = (own_current + own_difference * lag_blend_factor).astype(jnp.bfloat16)
    own_inner = jnp.tanh(dot32(blended, blending_lower_matrix)).astype(jnp.bfloat16)
    own_decay_mix = mix(
        own_current,
        own_difference,
        constant_lag_blends[0],
        own_inner[:, :inner_width],
        blending_raise_matrix[0],
    )
    own_decay_inner = jnp.tanh(dot32(own_decay_mix, fading_lower_matrix)).astype(jnp.bfloat16)
    own_narrow = jnp.concatenate([own_inner, own_decay_inner], axis=1)
    narrow_width = own_narrow.shape[1]
    narrow_rows = own_tokens * narrow_width // col_width

    def by_columns(rows):
        return rows.reshape(-1, row_groups, col_width).transpose(1, 0, 2)

    packed = jnp.concatenate(
        [
            by_columns(guess_vectors.reshape(own_tokens, width)),
            by_columns(preceding_symbol_vector),
            jnp.broadcast_to(
                own_narrow.reshape(1, narrow_rows, col_width),
                (row_groups, narrow_rows, col_width),
            ),
        ],
        axis=1,
    )
    packed = lax.all_to_all(packed, "dp", split_axis=0, concat_axis=0, tiled=True)
    packed = lax.all_gather(packed, "mp", axis=0, tiled=False)
    packed = packed.transpose(1, 0, 2, 3)
    tokens = packed[:, :, :own_tokens].reshape(
        row_groups, group_count, own_reqs, draft, col_width
    )
    edges = packed[:, :, own_tokens : own_tokens + own_reqs]
    narrow = packed[:, :, own_tokens + own_reqs :].reshape(
        row_groups, group_count * own_tokens, narrow_width
    )
    all_tokens = row_groups * group_count * own_tokens
    current, difference = shift(tokens, edges)
    current = current.reshape(all_tokens, col_width)
    difference = difference.reshape(all_tokens, col_width)
    inner_all = narrow.reshape(all_tokens, narrow_width)
    col_start = row_index * col_width
    constants = lax.dynamic_slice_in_dim(constant_lag_blends, col_start, col_width, 1)
    raises = lax.dynamic_slice_in_dim(blending_raise_matrix, col_start, col_width, 2)

    def partial(component, matrix):
        mixed = mix(
            current,
            difference,
            constants[component],
            inner_all[:, component * inner_width : (component + 1) * inner_width],
            raises[component],
        )
        return dot32(mixed, matrix).astype(jnp.bfloat16)

    def summed(values):
        return lax.psum_scatter(values, "dp", scatter_dimension=0, tiled=True).astype(jnp.float32)

    token_rows = row_reqs * draft
    pair = jnp.concatenate([partial(1, lookup_matrix), partial(2, payload_matrix)], axis=1)
    acceptor_matrix, gating_matrix, pair = lax.optimization_barrier(
        (acceptor_matrix, gating_matrix, pair)
    )
    lookup_vectors, payload_vectors = jnp.split(summed(pair), 2, axis=1)
    late_sum = lax.psum_scatter(
        jnp.concatenate([partial(3, acceptor_matrix), partial(4, gating_matrix)], axis=1),
        "dp",
        scatter_dimension=0,
        tiled=True,
    )
    row_narrow = lax.dynamic_index_in_dim(narrow, row_index, 0, keepdims=False)
    decay_inner_rows = row_narrow[:, narrow_width - decay_width :]
    logarithmic_fading_entries = -jnp.exp(
        constant_fading + dot32(decay_inner_rows, fading_raise_matrix)
    )

    def to_heads(values):
        return values.reshape(row_reqs, draft, local_heads, GROUP_DIMENSION)

    row_accepted = lax.dynamic_slice_in_dim(approved_guesses, row_index * row_reqs, row_reqs)
    lookup_heads, payload_heads = to_heads(lookup_vectors), to_heads(payload_vectors)
    cumulative, starts = fading_sums(to_heads(logarithmic_fading_entries))
    picked = picked_states(
        lookup_heads, payload_heads, cumulative, starts, earlier_memory_matrix, row_accepted
    )
    own_start = (row_index * group_count + group_index) * own_reqs
    own_accepted = lax.dynamic_slice_in_dim(approved_guesses, own_start, own_reqs)
    edge_rows = jnp.concatenate([preceding_symbol_vector[:, None, :], guess_vectors], axis=1)
    own_chosen = jnp.take_along_axis(edge_rows, own_accepted[:, None, None], axis=1)[:, 0]
    row_chosen = lax.all_gather(own_chosen, "mp", axis=0, tiled=True)
    chosen_cols = lax.all_gather(
        lax.dynamic_slice_in_dim(row_chosen, group_index * local_width, local_width, 1),
        "dp",
        axis=0,
        tiled=True,
    )
    capacity = 2 * row_reqs // row_groups
    target_rows = (destination_slot // row_reqs).reshape(row_groups, row_reqs)
    onehot = (
        target_rows[:, :, None] == jnp.arange(row_groups, dtype=jnp.int32)[None, None, :]
    ).astype(jnp.int32)
    earlier = jnp.cumsum(onehot, axis=1) - onehot
    ranks = jnp.sum(earlier * onehot, axis=-1)
    my_targets = lax.dynamic_index_in_dim(target_rows, row_index, 0, keepdims=False)
    my_ranks = lax.dynamic_index_in_dim(ranks, row_index, 0, keepdims=False)
    selected = (
        my_targets[:, None, None] == jnp.arange(row_groups, dtype=jnp.int32)[None, :, None]
    ) & (my_ranks[:, None, None] == jnp.arange(capacity, dtype=jnp.int32)[None, None, :])
    source_index = jnp.sum(
        selected.astype(jnp.int32) * jnp.arange(row_reqs, dtype=jnp.int32)[:, None, None], axis=0
    )
    send_state = picked.astype(jnp.bfloat16)[source_index]
    send_state, chosen_cols = lax.optimization_barrier((send_state, chosen_cols))
    recv_state = lax.all_to_all(send_state, "dp", split_axis=0, concat_axis=0, tiled=True)
    late_sum, send_state = lax.optimization_barrier((late_sum, send_state))
    acceptor_vectors, gate_raw = jnp.split(late_sum.astype(jnp.float32), 2, axis=1)
    outputs = wkv_blocks(
        to_heads(acceptor_vectors),
        lookup_heads,
        payload_heads,
        cumulative,
        starts,
        diagonal_boost,
        earlier_memory_matrix,
    )
    hidden = gated_norm(
        outputs.reshape(token_rows, local_heads, GROUP_DIMENSION),
        gate_raw,
        groupwise_scaling_factor,
        groupwise_scaling_offset,
    )
    emission_matrix, late_sum = lax.optimization_barrier((emission_matrix, late_sum))
    out_cols = lax.all_gather(emission_matrix, "dp", axis=1, tiled=True)
    attended = lax.psum_scatter(
        jnp.dot(hidden, out_cols, preferred_element_type=jnp.float32).astype(jnp.bfloat16),
        "mp",
        scatter_dimension=0,
        tiled=True,
    ).astype(jnp.float32)
    own_lengths = lax.dynamic_slice_in_dim(usable_guess_amount, own_start, own_reqs)
    valid_mask = jnp.arange(draft, dtype=jnp.int32)[None, :] < own_lengths[:, None]
    layer_out = (
        guess_vectors.astype(jnp.float32)
        + jnp.where(
            valid_mask[..., None],
            attended.reshape(own_reqs, draft, width),
            jnp.zeros((), jnp.float32),
        )
    ).astype(jnp.bfloat16)
    wanted = row_index * row_reqs + jnp.arange(row_reqs, dtype=jnp.int32)
    total_reqs = destination_slot.shape[0]
    matches = (destination_slot[None, :] == wanted[:, None]).astype(jnp.int32)
    which = jnp.sum(matches * jnp.arange(total_reqs, dtype=jnp.int32)[None, :], axis=1)
    flat_index = which // row_reqs * capacity + ranks.reshape(-1)[which]
    next_state = recv_state.reshape(
        row_groups * capacity, local_heads, GROUP_DIMENSION, GROUP_DIMENSION
    )[flat_index].astype(jnp.float32)
    next_edge = chosen_cols[which]
    return (layer_out, next_state, next_edge)


def solution(mesh):
    in_specs = (
        P(("dp", "mp"), None, None),
        P(("dp", "mp"), None),
        P("dp", "mp", None, None),
        P(),
        P(),
        P(),
        P(),
        P("mp"),
        P(),
        P(None, "mp"),
        P("mp", None),
        P("dp", "mp"),
        P("dp", "mp"),
        P("dp", "mp"),
        P("dp", "mp"),
        P("mp", "dp"),
        P("mp"),
        P("mp"),
        P(),
        P(),
        P(),
    )
    out_specs = (P(("dp", "mp"), None, None), P("dp", "mp", None, None), P("dp", "mp"))
    return jax.shard_map(
        on_device, mesh=mesh, in_specs=in_specs, out_specs=out_specs, check_vma=False
    )
```

```python
import jax
import jax.numpy as jnp
from jax import lax
from jax.sharding import PartitionSpec as P

GROUP_DIMENSION = 64


norm_eps = 0.00064


def shift(guess_vectors, edges):
    previous = jnp.concatenate([edges[..., None, :], guess_vectors[..., :-1, :]], axis=-2)
    current_input = guess_vectors.astype(jnp.float32)
    return current_input, previous.astype(jnp.float32) - current_input


def dot32(left, right):
    return jnp.dot(left, right, preferred_element_type=jnp.float32)


def mix(current_input, shift_difference, constant, inner, raise_matrix):
    return (current_input + shift_difference * (constant + dot32(inner, raise_matrix))).astype(
        jnp.bfloat16
    )


def fading_sums(logarithmic_fading_entries):
    cumulative = jnp.cumsum(logarithmic_fading_entries, axis=1)
    starts = jnp.concatenate(
        [jnp.zeros_like(logarithmic_fading_entries[:, :1]), cumulative], axis=1
    )
    return cumulative, starts


def picked_states(
    lookup_vectors, payload_vectors, cumulative, starts, starting_memory, approved_guesses
):
    draft = lookup_vectors.shape[1]
    at_accept = jnp.take_along_axis(starts, approved_guesses[:, None, None, None], axis=1)[:, 0]
    used = jnp.arange(draft)[None, :] < approved_guesses[:, None]
    coef_exp = jnp.where(used[:, :, None, None], at_accept[:, None] - cumulative, -1e30)
    weighted = jnp.exp(coef_exp) * lookup_vectors
    return jnp.exp(at_accept)[..., None] * starting_memory + jnp.einsum(
        "bshi,bshj->bhij", weighted, payload_vectors, precision=lax.Precision.HIGHEST
    )


def wkv_blocks(
    acceptor_vectors,
    lookup_vectors,
    payload_vectors,
    cumulative,
    starts,
    diagonal_boost,
    starting_memory,
):
    draft = acceptor_vectors.shape[1]
    before = starts[:, :draft]
    from_start = jnp.einsum(
        "bthi,bhij->bthj",
        acceptor_vectors * jnp.exp(before),
        starting_memory,
        precision=lax.Precision.HIGHEST,
    )
    later = jnp.arange(draft)[:, None] > jnp.arange(draft)[None, :]
    exponent = before[:, :, None] - cumulative[:, None, :]
    exponent = jnp.where(later[None, :, :, None, None], exponent, -1e30)
    scores = jnp.sum(
        acceptor_vectors[:, :, None] * lookup_vectors[:, None, :] * jnp.exp(exponent), axis=-1
    )
    inner = jnp.einsum("btsh,bshj->bthj", scores, payload_vectors, precision=lax.Precision.HIGHEST)
    diagonal_boost_contribution = (
        jnp.sum(acceptor_vectors * diagonal_boost * lookup_vectors, axis=-1, keepdims=True)
        * payload_vectors
    )
    return from_start + inner + diagonal_boost_contribution


def gated_norm(outputs, gate_raw, gain, bias):
    centre = jnp.mean(outputs, axis=-1, keepdims=True)
    spread = outputs - centre
    variance = jnp.mean(spread * spread, axis=-1, keepdims=True)
    normed = (spread * lax.rsqrt(variance + norm_eps)).reshape(outputs.shape[0], -1)
    return ((normed * gain + bias) * jax.nn.silu(gate_raw)).astype(jnp.bfloat16)


def on_device(
    guess_vectors,
    preceding_symbol_vector,
    earlier_memory_matrix,
    lag_blend_factor,
    constant_lag_blends,
    blending_lower_matrix,
    blending_raise_matrix,
    constant_fading,
    fading_lower_matrix,
    fading_raise_matrix,
    diagonal_boost,
    acceptor_matrix,
    lookup_matrix,
    payload_matrix,
    gating_matrix,
    emission_matrix,
    groupwise_scaling_factor,
    groupwise_scaling_offset,
    usable_guess_amount,
    approved_guesses,
    destination_slot,
):
    own_reqs, draft, width = guess_vectors.shape
    group_count = lax.axis_size("mp")
    row_groups = lax.axis_size("dp")
    row_reqs = own_reqs * group_count
    row_index = lax.axis_index("dp")
    group_index = lax.axis_index("mp")
    local_width = acceptor_matrix.shape[1]
    local_heads = local_width // GROUP_DIMENSION
    inner_width = blending_raise_matrix.shape[1]
    decay_width = fading_lower_matrix.shape[1]
    own_tokens = own_reqs * draft
    col_width = width // row_groups
    own_current, own_difference = shift(guess_vectors, preceding_symbol_vector)
    own_current = own_current.reshape(own_tokens, width)
    own_difference = own_difference.reshape(own_tokens, width)
    blended = (own_current + own_difference * lag_blend_factor).astype(jnp.bfloat16)
    own_inner = jnp.tanh(dot32(blended, blending_lower_matrix)).astype(jnp.bfloat16)
    own_decay_mix = mix(
        own_current,
        own_difference,
        constant_lag_blends[0],
        own_inner[:, :inner_width],
        blending_raise_matrix[0],
    )
    own_decay_inner = jnp.tanh(dot32(own_decay_mix, fading_lower_matrix)).astype(jnp.bfloat16)
    own_narrow = jnp.concatenate([own_inner, own_decay_inner], axis=1)
    narrow_width = own_narrow.shape[1]
    narrow_rows = own_tokens * narrow_width // col_width

    def by_columns(rows):
        return rows.reshape(-1, row_groups, col_width).transpose(1, 0, 2)

    packed = jnp.concatenate(
        [
            by_columns(guess_vectors.reshape(own_tokens, width)),
            by_columns(preceding_symbol_vector),
            jnp.broadcast_to(
                own_narrow.reshape(1, narrow_rows, col_width),
                (row_groups, narrow_rows, col_width),
            ),
        ],
        axis=1,
    )
    packed = lax.all_to_all(packed, "dp", split_axis=0, concat_axis=0, tiled=True)
    packed = lax.all_gather(packed, "mp", axis=0, tiled=False)
    packed = packed.transpose(1, 0, 2, 3)
    tokens = packed[:, :, :own_tokens].reshape(
        row_groups, group_count, own_reqs, draft, col_width
    )
    edges = packed[:, :, own_tokens : own_tokens + own_reqs]
    narrow = packed[:, :, own_tokens + own_reqs :].reshape(
        row_groups, group_count * own_tokens, narrow_width
    )
    all_tokens = row_groups * group_count * own_tokens
    current, difference = shift(tokens, edges)
    current = current.reshape(all_tokens, col_width)
    difference = difference.reshape(all_tokens, col_width)
    inner_all = narrow.reshape(all_tokens, narrow_width)
    col_start = row_index * col_width
    constants = lax.dynamic_slice_in_dim(constant_lag_blends, col_start, col_width, 1)
    raises = lax.dynamic_slice_in_dim(blending_raise_matrix, col_start, col_width, 2)

    def partial(component, matrix):
        mixed = mix(
            current,
            difference,
            constants[component],
            inner_all[:, component * inner_width : (component + 1) * inner_width],
            raises[component],
        )
        return dot32(mixed, matrix).astype(jnp.bfloat16)

    def summed(values):
        return lax.psum_scatter(values, "dp", scatter_dimension=0, tiled=True).astype(jnp.float32)

    token_rows = row_reqs * draft
    pair = jnp.concatenate([partial(1, lookup_matrix), partial(2, payload_matrix)], axis=1)
    acceptor_matrix, gating_matrix, pair = lax.optimization_barrier(
        (acceptor_matrix, gating_matrix, pair)
    )
    lookup_vectors, payload_vectors = jnp.split(summed(pair), 2, axis=1)
    late_sum = lax.psum_scatter(
        jnp.concatenate([partial(3, acceptor_matrix), partial(4, gating_matrix)], axis=1),
        "dp",
        scatter_dimension=0,
        tiled=True,
    )
    row_narrow = lax.dynamic_index_in_dim(narrow, row_index, 0, keepdims=False)
    decay_inner_rows = row_narrow[:, narrow_width - decay_width :]
    logarithmic_fading_entries = -jnp.exp(
        constant_fading + dot32(decay_inner_rows, fading_raise_matrix)
    )

    def to_heads(values):
        return values.reshape(row_reqs, draft, local_heads, GROUP_DIMENSION)

    row_accepted = lax.dynamic_slice_in_dim(approved_guesses, row_index * row_reqs, row_reqs)
    lookup_heads, payload_heads = to_heads(lookup_vectors), to_heads(payload_vectors)
    cumulative, starts = fading_sums(to_heads(logarithmic_fading_entries))
    picked = picked_states(
        lookup_heads, payload_heads, cumulative, starts, earlier_memory_matrix, row_accepted
    )
    own_start = (row_index * group_count + group_index) * own_reqs
    own_accepted = lax.dynamic_slice_in_dim(approved_guesses, own_start, own_reqs)
    edge_rows = jnp.concatenate([preceding_symbol_vector[:, None, :], guess_vectors], axis=1)
    own_chosen = jnp.take_along_axis(edge_rows, own_accepted[:, None, None], axis=1)[:, 0]
    row_chosen = lax.all_gather(own_chosen, "mp", axis=0, tiled=True)
    chosen_cols = lax.all_gather(
        lax.dynamic_slice_in_dim(row_chosen, group_index * local_width, local_width, 1),
        "dp",
        axis=0,
        tiled=True,
    )
    capacity = 2 * row_reqs // row_groups
    target_rows = (destination_slot // row_reqs).reshape(row_groups, row_reqs)
    onehot = (
        target_rows[:, :, None] == jnp.arange(row_groups, dtype=jnp.int32)[None, None, :]
    ).astype(jnp.int32)
    earlier = jnp.cumsum(onehot, axis=1) - onehot
    ranks = jnp.sum(earlier * onehot, axis=-1)
    my_targets = lax.dynamic_index_in_dim(target_rows, row_index, 0, keepdims=False)
    my_ranks = lax.dynamic_index_in_dim(ranks, row_index, 0, keepdims=False)
    selected = (
        my_targets[:, None, None] == jnp.arange(row_groups, dtype=jnp.int32)[None, :, None]
    ) & (my_ranks[:, None, None] == jnp.arange(capacity, dtype=jnp.int32)[None, None, :])
    source_index = jnp.sum(
        selected.astype(jnp.int32) * jnp.arange(row_reqs, dtype=jnp.int32)[:, None, None], axis=0
    )
    send_state = picked.astype(jnp.bfloat16)[source_index].reshape(
        row_groups, capacity, local_heads * GROUP_DIMENSION * GROUP_DIMENSION // 128, 128
    )
    send_state, chosen_cols = lax.optimization_barrier((send_state, chosen_cols))
    recv_state = lax.all_to_all(send_state, "dp", split_axis=0, concat_axis=0, tiled=True)
    late_sum, send_state = lax.optimization_barrier((late_sum, send_state))
    acceptor_vectors, gate_raw = jnp.split(late_sum.astype(jnp.float32), 2, axis=1)
    outputs = wkv_blocks(
        to_heads(acceptor_vectors),
        lookup_heads,
        payload_heads,
        cumulative,
        starts,
        diagonal_boost,
        earlier_memory_matrix,
    )
    hidden = gated_norm(
        outputs.reshape(token_rows, local_heads, GROUP_DIMENSION),
        gate_raw,
        groupwise_scaling_factor,
        groupwise_scaling_offset,
    )
    emission_matrix, late_sum = lax.optimization_barrier((emission_matrix, late_sum))
    out_cols = lax.all_gather(emission_matrix, "dp", axis=1, tiled=True)
    attended = lax.psum_scatter(
        jnp.dot(hidden, out_cols, preferred_element_type=jnp.float32).astype(jnp.bfloat16),
        "mp",
        scatter_dimension=0,
        tiled=True,
    ).astype(jnp.float32)
    own_lengths = lax.dynamic_slice_in_dim(usable_guess_amount, own_start, own_reqs)
    valid_mask = jnp.arange(draft, dtype=jnp.int32)[None, :] < own_lengths[:, None]
    layer_out = (
        guess_vectors.astype(jnp.float32)
        + jnp.where(
            valid_mask[..., None],
            attended.reshape(own_reqs, draft, width),
            jnp.zeros((), jnp.float32),
        )
    ).astype(jnp.bfloat16)
    wanted = row_index * row_reqs + jnp.arange(row_reqs, dtype=jnp.int32)
    total_reqs = destination_slot.shape[0]
    matches = (destination_slot[None, :] == wanted[:, None]).astype(jnp.int32)
    which = jnp.sum(matches * jnp.arange(total_reqs, dtype=jnp.int32)[None, :], axis=1)
    flat_index = which // row_reqs * capacity + ranks.reshape(-1)[which]
    next_state = (
        recv_state.reshape(row_groups * capacity, -1, 128)[flat_index]
        .reshape(row_reqs, local_heads, GROUP_DIMENSION, GROUP_DIMENSION)
        .astype(jnp.float32)
    )
    next_edge = chosen_cols[which]
    return (layer_out, next_state, next_edge)


def solution(mesh):
    in_specs = (
        P(("dp", "mp"), None, None),
        P(("dp", "mp"), None),
        P("dp", "mp", None, None),
        P(),
        P(),
        P(),
        P(),
        P("mp"),
        P(),
        P(None, "mp"),
        P("mp", None),
        P("dp", "mp"),
        P("dp", "mp"),
        P("dp", "mp"),
        P("dp", "mp"),
        P("mp", "dp"),
        P("mp"),
        P("mp"),
        P(),
        P(),
        P(),
    )
    out_specs = (P(("dp", "mp"), None, None), P("dp", "mp", None, None), P("dp", "mp"))
    return jax.shard_map(
        on_device, mesh=mesh, in_specs=in_specs, out_specs=out_specs, check_vma=False
    )
```
